1024 devices in a mesh: dp: 128 (over x, y, core), tp: 8 (over z).
Axes of the slice: x: 8, y: 8, z: 8, core: 2. Of those that a mesh axis runs over, the one named last changes fastest.
Arguments:
- normed: bfloat16 [128, 768, 4096], P('dp', 'tp'), may hold values from -6 to 6
- key_grad: bfloat16 [128, 768, 1024], P('dp', None, 'tp'), may hold values from -0.18 to 0.18
- error_in: bfloat16 [128, 4096, 1024], P('dp', None, 'tp'), may hold values from -3 to 3
- q_init: float32 [1024, 32], P('tp'), may hold values from -6 to 6
Outputs:
- error_next: bfloat16 [128, 4096, 1024], P('dp', None, 'tp')
- p_basis: float32 [4096, 32], replicated
- q_mean: float32 [1024, 32], P('tp')
The draws below stay inside these ranges and needn't reach their ends.
All inputs are finite; a program needn't handle non-finite values.
Results may differ from the reference program's by a relative error of at most 0.007.
Values may be sent and summed in bfloat16 or wider, within the bound.
No kernel may reach another device: no remote copies, remote signals or barrier semaphores. Data moves between devices by JAX's collectives and lax.ppermute only.
A program may use at most 32 MiB of HBM per device.

```python
import jax
import jax.numpy as jnp
from jax import lax

D_WIN = 4096
RANK = 32
TOK = 768
KW = 1024
N_DP = 128


def token_parts(key):
    first, second = jax.random.split(key)
    groups = max(RANK // 2, 1)
    directions = jax.random.randint(first, (N_DP, TOK), 0, groups).astype(jnp.int32)
    weights = jax.random.uniform(second, (N_DP, TOK), jnp.float32, 0.5, 1.5)
    return (directions, weights)


def draw_normed(key, part):
    directions, weights = token_parts(key)
    key = jax.random.fold_in(key, 1)
    groups = max(RANK // 2, 1)
    basis_key, noise_key = jax.random.split(key)
    basis = jnp.clip(jax.random.normal(basis_key, (groups, D_WIN), jnp.float32), -3.0, 3.0)
    amplitude = 0.8
    strength = (amplitude * (groups / TOK) ** 0.5) ** 0.5

    def replica(index):
        replica_key = jax.random.fold_in(noise_key, index)
        noise = jnp.clip(jax.random.normal(replica_key, (TOK, D_WIN), jnp.float32), -4.0, 4.0)
        planted = jnp.take(basis, directions[index], axis=0)
        return jnp.clip(noise + strength * weights[index][:, None] * planted, -6.0, 6.0)
    return lax.map(replica, jnp.arange(N_DP, dtype=jnp.int32)).astype(jnp.bfloat16)


def draw_key_grad(key, part):
    directions, weights = token_parts(key)
    key = jax.random.fold_in(key, 2)
    groups = max(RANK // 2, 1)
    basis_key, noise_key = jax.random.split(key)
    basis = jnp.clip(jax.random.normal(basis_key, (groups, KW), jnp.float32), -3.0, 3.0)
    amplitude = 0.8
    strength = (amplitude * (groups / TOK) ** 0.5) ** 0.5

    def replica(index):
        replica_key = jax.random.fold_in(noise_key, index)
        noise = jnp.clip(jax.random.normal(replica_key, (TOK, KW), jnp.float32), -4.0, 4.0)
        planted = jnp.take(basis, directions[index], axis=0)
        return jnp.clip(0.03 * (noise + strength * weights[index][:, None] * planted), -0.18, 0.18)
    return lax.map(replica, jnp.arange(N_DP, dtype=jnp.int32)).astype(jnp.bfloat16)


def shard_levels(stream_key, extent, cuts, least, largest):
    def one(axis_at, parts):
        draws = jax.random.uniform(jax.random.fold_in(jax.random.fold_in(stream_key, 6), axis_at), (parts,), jnp.float32, least / len(cuts), largest / len(cuts))
        return jnp.repeat(jnp.exp(draws), extent[axis_at] // parts).reshape((-1,) + (1,) * (len(extent) - axis_at - 1))

    loudness = one(*cuts[0])
    for cut in cuts[1:]:
        loudness = loudness * one(*cut)
    return loudness


def scatter_about(rng, dims, spread, reach, cuts=(), kind=jnp.bfloat16):
    entries = jax.random.normal(rng, dims, jnp.float32) * spread
    if len(cuts) > 0:
        entries = shard_levels(rng, dims, cuts, -0.22, 0.18) * entries
    return jnp.clip(entries, min=-reach, max=reach).astype(kind)


def setup_inputs(seed: int = 0) -> dict:
    keys = jax.random.split(jax.random.key(seed), 5)
    return {
        "normed": draw_normed(jax.random.fold_in(keys[4], 71), 0),
        "key_grad": draw_key_grad(jax.random.fold_in(keys[4], 71), 0),
        "error_in": scatter_about(keys[2], (N_DP, D_WIN, KW), 0.5, 3.0, ((0, 128), (2, 8))),
        "q_init": scatter_about(keys[3], (KW, RANK), 1.0, 6.0, ((0, 8),), jnp.float32),
    }


def orthonormal(p_sum):
    gram = jnp.dot(p_sum.T, p_sum, precision=lax.Precision.HIGHEST)
    lower = jnp.linalg.cholesky(gram)
    return lax.linalg.triangular_solve(lower, p_sum, left_side=False, lower=True, transpose_a=True)

def reference(normed, key_grad, error_in, q_init):
    high = lax.Precision.HIGHEST

    def p_term(total, items):
        inputs, grads, errors = items
        inputs = inputs.astype(jnp.float32)
        grads = grads.astype(jnp.float32)
        part = jnp.dot(inputs.T, jnp.dot(grads, q_init, precision=high), precision=high)
        part = part + jnp.dot(errors.astype(jnp.float32), q_init, precision=high)
        return (total + part, None)
    start = jnp.zeros((normed.shape[2], q_init.shape[1]), jnp.float32)
    p_sum, _ = lax.scan(p_term, start, (normed, key_grad, error_in))
    p_basis = orthonormal(p_sum)

    def q_term(total, items):
        inputs, grads, errors = items
        inputs = inputs.astype(jnp.float32)
        grads = grads.astype(jnp.float32)
        part = jnp.dot(grads.T, jnp.dot(inputs, p_basis, precision=high), precision=high)
        part = part + jnp.dot(errors.astype(jnp.float32).T, p_basis, precision=high)
        return (total + part, None)
    qstart = jnp.zeros(q_init.shape, jnp.float32)
    q_sum, _ = lax.scan(q_term, qstart, (normed, key_grad, error_in))
    q_mean = q_sum / normed.shape[0]
    approx = jnp.dot(p_basis, q_mean.T, precision=high)

    def error_step(carry, items):
        inputs, grads, errors = items
        merged = jnp.dot(inputs.astype(jnp.float32).T, grads.astype(jnp.float32), precision=high)
        merged = merged + errors.astype(jnp.float32)
        return (carry, (merged - approx).astype(jnp.bfloat16))
    _, error_next = lax.scan(error_step, 0.0, (normed, key_grad, error_in))
    return (error_next, p_basis, q_mean)
```

```python
import math

import jax
import jax.numpy as jnp
from jax import lax
from jax.sharding import Mesh, PartitionSpec as P

F32 = jnp.float32
BF16 = jnp.bfloat16
HIGH = lax.Precision.HIGHEST
PLANE = ("x", "y")


def two_terms(value):
    head = lax.reduce_precision(value, 8, 7)
    return jnp.concatenate([head.astype(BF16), (value - head).astype(BF16)], axis=0)


def fold(value):
    half = value.shape[0] // 2
    return value[:half] + value[half:]


def swap(value, axes):
    return lax.all_to_all(value, axes, 0, 0, tiled=True)


def spread(value, axes):
    return swap(jnp.broadcast_to(value[None], (lax.axis_size(axes),) + value.shape), axes)


def on_device(normed, key_grad, error_in, q_init):
    inputs, grads, errors = normed[0], key_grad[0], error_in[0]
    tp = lax.axis_size("z")
    plane = lax.axis_size(PLANE)
    replicas = plane * lax.axis_size("c")
    tokens, wide = inputs.shape
    rank = q_init.shape[1]
    gathered = lax.all_gather(inputs, "z", axis=0, tiled=True)

    q_terms = two_terms(q_init.T)
    by_head = fold(lax.dot_general(q_terms, grads, (((1,), (1,)), ((), ())), preferred_element_type=F32))
    by_token = jnp.transpose(by_head.reshape(rank, tp, tokens), (1, 0, 2))
    mine = jnp.sum(swap(by_token, "z"), axis=0)

    p_local = jnp.dot(two_terms(mine), inputs, preferred_element_type=F32)
    p_local += lax.dot_general(q_terms, errors, (((1,), (1,)), ((), ())), preferred_element_type=F32)
    p_local = fold(p_local)
    lanes = 128
    columns = wide // lanes
    halves = plane // columns
    depth = rank // halves
    pieces = jnp.transpose(p_local.reshape(halves, depth, columns, lanes), (0, 2, 1, 3))
    pieces = pieces.reshape(plane, depth, lanes).astype(BF16)
    piece = jnp.sum(swap(pieces, PLANE).astype(F32), axis=0)
    piece = jnp.sum(spread(piece, ("c", "z")), axis=0)
    p_sum = spread(piece, PLANE).reshape(halves, columns, depth, lanes)
    p_sum = jnp.transpose(p_sum, (0, 2, 1, 3)).reshape(rank, wide)

    gram = lax.dot_general(p_sum, p_sum, (((1,), (1,)), ((), ())), precision=HIGH)
    lower = jnp.linalg.cholesky(gram)
    inverse = lax.linalg.triangular_solve(lower, jnp.eye(rank, dtype=F32), left_side=True, lower=True)
    p_basis = jnp.dot(inverse, p_sum, precision=HIGH)

    merged = lax.dot_general(gathered, grads, (((0,), (0,)), ((), ())), preferred_element_type=F32)
    merged = merged + errors.astype(F32)
    q_local = jnp.dot(p_basis, merged, precision=HIGH)
    q_local = q_local + lax.ppermute(q_local, "c", [(0, 1), (1, 0)])
    q_mean = jnp.sum(spread(q_local.astype(BF16), PLANE).astype(F32), axis=0) / replicas
    approx = lax.dot_general(p_basis, q_mean, (((0,), (0,)), ((), ())), precision=HIGH)
    error_next = (merged - approx).astype(BF16)[None]
    return (error_next, p_basis.T, q_mean.T)


def solution(mesh):
    side = math.isqrt(mesh.shape["dp"] // 2)
    whole = Mesh(mesh.devices.reshape(side, side, 2, mesh.shape["tp"]), ("x", "y", "c", "z"))
    dp = ("x", "y", "c")
    placed = (P(dp, "z", None), P(dp, None, "z"), P(dp, None, "z"), P("z", None))
    return jax.shard_map(
        on_device,
        mesh=whole,
        in_specs=placed,
        out_specs=(P(dp, None, "z"), P(), P("z", None)),
        check_vma=False,
    )
```

```python
import functools
import math

import jax
import jax.numpy as jnp
from jax import lax
from jax.experimental import pallas as pl
from jax.experimental.pallas import tpu as pltpu
from jax.sharding import Mesh, PartitionSpec as P

F32 = jnp.float32
BF16 = jnp.bfloat16
HIGH = lax.Precision.HIGHEST
PLANE = ("x", "y")
ROWS = ((1,), (1,))
COLUMNS = ((0,), (0,))
PLAIN = ((1,), (0,))


def two_terms(value):
    head = lax.reduce_precision(value, 8, 7)
    return jnp.concatenate([head.astype(BF16), (value - head).astype(BF16)], axis=0)


def fold(value):
    half = value.shape[0] // 2
    return value[:half] + value[half:]


def swap(value, axes):
    return lax.all_to_all(value, axes, 0, 0, tiled=True)


def spread(value, axes):
    return swap(jnp.broadcast_to(value[None], (lax.axis_size(axes),) + value.shape), axes)


def dot(a, b, axes=PLAIN):
    return lax.dot_general(a, b, (axes, ((), ())), preferred_element_type=F32)


def split(value):
    head = value.astype(BF16)
    return head, (value - head.astype(F32)).astype(BF16)


def merge_body(inputs, grads, errors, basis, merged, q_out, turned):
    @pl.when(pl.program_id(0) == 0)
    def _():
        q_out[...] = jnp.zeros_like(q_out)
        turned[...] = grads[...].T

    block = dot(turned[...], inputs[...]).T + errors[...].astype(F32)
    merged[...] = block
    high, low = split(block)
    b_high, b_low = split(basis[...])
    rank = b_high.shape[0]
    q = dot(jnp.concatenate([b_high, b_low], axis=0), high)
    q_out[...] += q[:rank] + q[rank:] + dot(b_high, low)


def merge(inputs, grads, errors, basis, block):
    tokens, wide = inputs.shape
    cols, rank = grads.shape[1], basis.shape[0]
    return pl.pallas_call(
        merge_body,
        grid=(wide // block,),
        in_specs=[
            pl.BlockSpec((tokens, block), lambda i: (0, i)),
            pl.BlockSpec((tokens, cols), lambda i: (0, 0)),
            pl.BlockSpec((block, cols), lambda i: (i, 0)),
            pl.BlockSpec((rank, block), lambda i: (0, i)),
        ],
        out_specs=[
            pl.BlockSpec((block, cols), lambda i: (i, 0)),
            pl.BlockSpec((rank, cols), lambda i: (0, 0)),
        ],
        out_shape=[
            jax.ShapeDtypeStruct((wide, cols), F32),
            jax.ShapeDtypeStruct((rank, cols), F32),
        ],
        scratch_shapes=[pltpu.VMEM((cols, tokens), BF16)],
        compiler_params=pltpu.CompilerParams(vmem_limit_bytes=52 * 2**20),
        cost_estimate=pl.CostEstimate(
            flops=2 * tokens * wide * cols, bytes_accessed=2 * tokens * wide, transcendentals=0
        ),
        name="merge",
    )(inputs, grads, errors, basis)


def finish_body(scale, merged, basis, terms, error_next, q_mean, factors):
    @pl.when(pl.program_id(0) == 0)
    def _():
        mean = jnp.sum(terms[...], axis=0) * scale
        q_mean[...] = mean
        high, low = split(mean)
        factors[...] = jnp.concatenate([high, low, high], axis=0)

    high, low = split(basis[...])
    approx = dot(jnp.concatenate([high, high, low], axis=0), factors[...], COLUMNS)
    error_next[...] = (merged[...] - approx).astype(BF16)


def finish(merged, basis, terms, scale, block):
    wide, cols = merged.shape
    rank = basis.shape[0]
    return pl.pallas_call(
        functools.partial(finish_body, scale),
        grid=(wide // block,),
        in_specs=[
            pl.BlockSpec((block, cols), lambda i: (i, 0)),
            pl.BlockSpec((rank, block), lambda i: (0, i)),
            pl.BlockSpec(terms.shape, lambda i: (0, 0, 0)),
        ],
        out_specs=[
            pl.BlockSpec((block, cols), lambda i: (i, 0)),
            pl.BlockSpec((rank, cols), lambda i: (0, 0)),
        ],
        out_shape=[
            jax.ShapeDtypeStruct((wide, cols), BF16),
            jax.ShapeDtypeStruct((rank, cols), F32),
        ],
        scratch_shapes=[pltpu.VMEM((3 * rank, cols), BF16)],
        compiler_params=pltpu.CompilerParams(vmem_limit_bytes=24 * 2**20),
        cost_estimate=pl.CostEstimate(
            flops=6 * rank * wide * cols, bytes_accessed=6 * wide * cols, transcendentals=0
        ),
        name="finish",
    )(merged, basis, terms)


def on_device(normed, key_grad, error_in, q_init):
    inputs, grads, errors = normed[0], key_grad[0], error_in[0]
    tp = lax.axis_size("z")
    plane = lax.axis_size(PLANE)
    replicas = plane * lax.axis_size("c")
    tokens, wide = inputs.shape
    rank = q_init.shape[1]
    gathered = lax.all_gather(inputs, "z", axis=0, tiled=True)

    q_terms = two_terms(q_init.T)
    by_head = fold(lax.dot_general(q_terms, grads, (((1,), (1,)), ((), ())), preferred_element_type=F32))
    by_token = jnp.transpose(by_head.reshape(rank, tp, tokens), (1, 0, 2))
    mine = jnp.sum(swap(by_token, "z"), axis=0)

    p_local = jnp.dot(two_terms(mine), inputs, preferred_element_type=F32)
    p_local += lax.dot_general(q_terms, errors, (((1,), (1,)), ((), ())), preferred_element_type=F32)
    p_local = fold(p_local)
    lanes = 128
    columns = wide // lanes
    halves = plane // columns
    depth = rank // halves
    pieces = jnp.transpose(p_local.reshape(halves, depth, columns, lanes), (0, 2, 1, 3))
    pieces = pieces.reshape(plane, depth, lanes).astype(BF16)
    piece = jnp.sum(swap(pieces, PLANE).astype(F32), axis=0)
    piece = jnp.sum(spread(piece, ("c", "z")), axis=0)
    p_sum = spread(piece, PLANE).reshape(halves, columns, depth, lanes)
    p_sum = jnp.transpose(p_sum, (0, 2, 1, 3)).reshape(rank, wide)

    gram = lax.dot_general(p_sum, p_sum, (((1,), (1,)), ((), ())), precision=HIGH)
    lower = jnp.linalg.cholesky(gram)
    inverse = lax.linalg.triangular_solve(lower, jnp.eye(rank, dtype=F32), left_side=True, lower=True)
    p_basis = jnp.dot(inverse, p_sum, precision=HIGH)

    merged, q_local = merge(gathered, grads, errors, p_basis, 1024)
    q_local = q_local + lax.ppermute(q_local, "c", [(0, 1), (1, 0)])
    q_local = jnp.sum(spread(q_local, "x"), axis=0)
    error_next, q_mean = finish(merged, p_basis, spread(q_local, "y"), 1.0 / replicas, 2048)
    return (error_next[None], p_basis.T, q_mean.T)


def solution(mesh):
    side = math.isqrt(mesh.shape["dp"] // 2)
    whole = Mesh(mesh.devices.reshape(side, side, 2, mesh.shape["tp"]), ("x", "y", "c", "z"))
    dp = ("x", "y", "c")
    placed = (P(dp, "z", None), P(dp, None, "z"), P(dp, None, "z"), P("z", None))
    return jax.shard_map(
        on_device,
        mesh=whole,
        in_specs=placed,
        out_specs=(P(dp, None, "z"), P(), P("z", None)),
        check_vma=False,
    )
```

```python
import functools
import math

import jax
import jax.numpy as jnp
from jax import lax
from jax.experimental import pallas as pl
from jax.experimental.pallas import tpu as pltpu
from jax.sharding import Mesh, PartitionSpec as P

F32 = jnp.float32
BF16 = jnp.bfloat16
HIGH = lax.Precision.HIGHEST
PLANE = ("x", "y")
ROWS = ((1,), (1,))
COLUMNS = ((0,), (0,))
PLAIN = ((1,), (0,))


def two_terms(value):
    head = lax.reduce_precision(value, 8, 7)
    return jnp.concatenate([head.astype(BF16), (value - head).astype(BF16)], axis=0)


def fold(value):
    half = value.shape[0] // 2
    return value[:half] + value[half:]


def swap(value, axes):
    return lax.all_to_all(value, axes, 0, 0, tiled=True)


def spread(value, axes):
    return swap(jnp.broadcast_to(value[None], (lax.axis_size(axes),) + value.shape), axes)


def dot(a, b, axes=PLAIN):
    return lax.dot_general(a, b, (axes, ((), ())), preferred_element_type=F32)


def split(value):
    head = value.astype(BF16)
    return head, (value - head.astype(F32)).astype(BF16)


def merge_body(count, *refs):
    parts, (grads, errors, merged, turned) = refs[:count], refs[count:]

    @pl.when(pl.program_id(0) == 0)
    def _():
        turned[...] = grads[...].T

    inputs = jnp.concatenate([part[...] for part in parts], axis=0)
    merged[...] = dot(turned[...], inputs).T + errors[...].astype(F32)


def merge(parts, grads, errors, block):
    count = len(parts)
    rows, wide = parts[0].shape
    tokens, cols = grads.shape
    return pl.pallas_call(
        functools.partial(merge_body, count),
        grid=(wide // block,),
        in_specs=[pl.BlockSpec((rows, block), lambda i: (0, i)) for _ in parts]
        + [
            pl.BlockSpec((tokens, cols), lambda i: (0, 0)),
            pl.BlockSpec((block, cols), lambda i: (i, 0)),
        ],
        out_specs=pl.BlockSpec((block, cols), lambda i: (i, 0)),
        out_shape=jax.ShapeDtypeStruct((wide, cols), F32),
        scratch_shapes=[pltpu.VMEM((cols, tokens), BF16)],
        compiler_params=pltpu.CompilerParams(vmem_limit_bytes=24 * 2**20),
        cost_estimate=pl.CostEstimate(
            flops=2 * tokens * wide * cols, bytes_accessed=2 * tokens * wide, transcendentals=0
        ),
        name="merge",
    )(*parts, grads, errors)


def in_order(grads, axis, rows, order):
    size = lax.axis_size(axis)
    twice = jnp.concatenate([grads, grads], axis=0)
    turned = lax.dynamic_slice_in_dim(twice, lax.axis_index(axis) * rows, size * rows, axis=0)
    return jnp.concatenate([turned[(o % size) * rows : (o % size + 1) * rows] for o in order], axis=0)


def finish_body(scale, merged, basis, terms, error_next, q_mean, factors):
    @pl.when(pl.program_id(0) == 0)
    def _():
        mean = jnp.sum(terms[...].astype(F32), axis=0) * scale
        q_mean[...] = mean
        high, low = split(mean)
        factors[...] = jnp.concatenate([high, low, high], axis=0)

    high, low = split(basis[...])
    approx = dot(jnp.concatenate([high, high, low], axis=0), factors[...], COLUMNS)
    error_next[...] = (merged[...] - approx).astype(BF16)


def finish(merged, basis, terms, scale, block):
    wide, cols = merged.shape
    rank = basis.shape[0]
    return pl.pallas_call(
        functools.partial(finish_body, scale),
        grid=(wide // block,),
        in_specs=[
            pl.BlockSpec((block, cols), lambda i: (i, 0)),
            pl.BlockSpec((rank, block), lambda i: (0, i)),
            pl.BlockSpec(terms.shape, lambda i: (0, 0, 0)),
        ],
        out_specs=[
            pl.BlockSpec((block, cols), lambda i: (i, 0)),
            pl.BlockSpec((rank, cols), lambda i: (0, 0)),
        ],
        out_shape=[
            jax.ShapeDtypeStruct((wide, cols), BF16),
            jax.ShapeDtypeStruct((rank, cols), F32),
        ],
        scratch_shapes=[pltpu.VMEM((3 * rank, cols), BF16)],
        compiler_params=pltpu.CompilerParams(vmem_limit_bytes=24 * 2**20),
        cost_estimate=pl.CostEstimate(
            flops=6 * rank * wide * cols, bytes_accessed=6 * wide * cols, transcendentals=0
        ),
        name="finish",
    )(merged, basis, terms)


def on_device(normed, key_grad, error_in, q_init):
    inputs, grads, errors = normed[0], key_grad[0], error_in[0]
    tp = lax.axis_size("z")
    plane = lax.axis_size(PLANE)
    replicas = plane * lax.axis_size("c")
    tokens, wide = inputs.shape
    rank = q_init.shape[1]
    ahead = [(i, (i + 1) % tp) for i in range(tp)]
    back = [(i, (i - 1) % tp) for i in range(tp)]
    up, down, order = [inputs], [inputs], [0]
    for step in range(1, tp // 2 + 1):
        up.append(lax.ppermute(up[-1], "z", ahead))
        order.append(-step)
        if 2 * step < tp:
            down.append(lax.ppermute(down[-1], "z", back))
            order.append(step)
    parts = [inputs] + [p for pair in zip(up[1:], down[1:]) for p in pair] + up[len(down) :]

    q_terms = two_terms(q_init.T)
    by_head = fold(lax.dot_general(q_terms, grads, (((1,), (1,)), ((), ())), preferred_element_type=F32))
    by_token = jnp.transpose(by_head.reshape(rank, tp, tokens), (1, 0, 2))
    mine = jnp.sum(swap(by_token, "z"), axis=0)

    p_local = jnp.dot(two_terms(mine), inputs, preferred_element_type=F32)
    p_local += lax.dot_general(q_terms, errors, (((1,), (1,)), ((), ())), preferred_element_type=F32)
    p_local = fold(p_local)
    lanes = 128
    columns = wide // lanes
    halves = plane // columns
    depth = rank // halves
    pieces = jnp.transpose(p_local.reshape(halves, depth, columns, lanes), (0, 2, 1, 3))
    pieces = pieces.reshape(plane, depth, lanes)
    piece = jnp.sum(swap(pieces, PLANE), axis=0)
    piece = jnp.sum(spread(piece, ("c", "z")), axis=0)
    p_sum = spread(piece, PLANE).reshape(halves, columns, depth, lanes)
    p_sum = jnp.transpose(p_sum, (0, 2, 1, 3)).reshape(rank, wide)

    p_terms = two_terms(p_sum)
    met = fold(dot(p_terms, inputs, ROWS))
    met = spread(met, "z")
    q_raw = fold(dot(p_terms, errors))
    met = jnp.transpose(met, (1, 0, 2)).reshape(rank, tp * tokens)
    q_raw = q_raw + fold(dot(two_terms(met), grads))

    gram = lax.dot_general(p_sum, p_sum, (((1,), (1,)), ((), ())), precision=HIGH)
    lower = jnp.linalg.cholesky(gram)
    inverse = lax.linalg.triangular_solve(lower, jnp.eye(rank, dtype=F32), left_side=True, lower=True)
    p_basis = jnp.dot(inverse, p_sum, precision=HIGH)
    q_local = jnp.dot(inverse, q_raw, precision=HIGH)

    merged = merge(parts, in_order(grads, "z", tokens, order), errors, 1024)
    q_local = jnp.sum(spread(q_local, ("y", "c")), axis=0)
    error_next, q_mean = finish(merged, p_basis, spread(q_local, "x"), 1.0 / replicas, 2048)
    return (error_next[None], p_basis.T, q_mean.T)


def solution(mesh):
    side = math.isqrt(mesh.shape["dp"] // 2)
    whole = Mesh(mesh.devices.reshape(side, side, 2, mesh.shape["tp"]), ("x", "y", "c", "z"))
    dp = ("x", "y", "c")
    placed = (P(dp, "z", None), P(dp, None, "z"), P(dp, None, "z"), P("z", None))
    return jax.shard_map(
        on_device,
        mesh=whole,
        in_specs=placed,
        out_specs=(P(dp, None, "z"), P(), P("z", None)),
        check_vma=False,
    )
```

```python
import functools
import math

import jax
import jax.numpy as jnp
from jax import lax
from jax.experimental import pallas as pl
from jax.experimental.pallas import tpu as pltpu
from jax.sharding import Mesh, PartitionSpec as P

F32 = jnp.float32
BF16 = jnp.bfloat16
HIGH = lax.Precision.HIGHEST
PLANE = ("x", "y")
ROWS = ((1,), (1,))
COLUMNS = ((0,), (0,))
PLAIN = ((1,), (0,))


def two_terms(value):
    head = lax.reduce_precision(value, 8, 7)
    return jnp.concatenate([head.astype(BF16), (value - head).astype(BF16)], axis=0)


def fold(value):
    half = value.shape[0] // 2
    return value[:half] + value[half:]


def swap(value, axes):
    return lax.all_to_all(value, axes, 0, 0, tiled=True)


def spread(value, axes):
    return swap(jnp.broadcast_to(value[None], (lax.axis_size(axes),) + value.shape), axes)


def dot(a, b, axes=PLAIN):
    return lax.dot_general(a, b, (axes, ((), ())), preferred_element_type=F32)


def split(value):
    head = value.astype(BF16)
    return head, (value - head.astype(F32)).astype(BF16)


def factor_body(rows, inverse):
    value = rows[...]
    left = lax.dot_general(value, value, (ROWS, ((), ())), precision=HIGH, preferred_element_type=F32)
    rank = left.shape[0]
    row = lax.broadcasted_iota(jnp.int32, (rank, rank), 0)
    column = lax.broadcasted_iota(jnp.int32, (rank, rank), 1)
    right = jnp.where(row == column, 1.0, 0.0).astype(F32)
    for k in range(rank):
        scale = lax.rsqrt(left[k : k + 1, k : k + 1])
        upper = left[k : k + 1] * scale
        solved = right[k : k + 1] * scale
        if k + 1 < rank:
            below = jnp.where(row[:, :1] > k, left[:, k : k + 1] * scale, 0.0)
            left = left - below * upper
            right = right - below * solved
        right = jnp.where(row == k, solved, right)
    inverse[...] = right


def factor(rows):
    rank = rows.shape[0]
    return pl.pallas_call(
        factor_body,
        out_shape=jax.ShapeDtypeStruct((rank, rank), F32),
        compiler_params=pltpu.CompilerParams(vmem_limit_bytes=8 * 2**20),
        name="factor",
    )(rows)


def merge_body(inputs, grads, errors, basis, merged, q_out, turned):
    @pl.when(pl.program_id(0) == 0)
    def _():
        q_out[...] = jnp.zeros_like(q_out)
        turned[...] = grads[...].T

    block = dot(turned[...], inputs[...]).T + errors[...].astype(F32)
    merged[...] = block
    high, low = split(block)
    b_high, b_low = split(basis[...])
    rank = b_high.shape[0]
    q = dot(jnp.concatenate([b_high, b_low], axis=0), high)
    q_out[...] += q[:rank] + q[rank:] + dot(b_high, low)


def merge(inputs, grads, errors, basis, block):
    tokens, wide = inputs.shape
    cols, rank = grads.shape[1], basis.shape[0]
    return pl.pallas_call(
        merge_body,
        grid=(wide // block,),
        in_specs=[
            pl.BlockSpec((tokens, block), lambda i: (0, i)),
            pl.BlockSpec((tokens, cols), lambda i: (0, 0)),
            pl.BlockSpec((block, cols), lambda i: (i, 0)),
            pl.BlockSpec((rank, block), lambda i: (0, i)),
        ],
        out_specs=[
            pl.BlockSpec((block, cols), lambda i: (i, 0)),
            pl.BlockSpec((rank, cols), lambda i: (0, 0)),
        ],
        out_shape=[
            jax.ShapeDtypeStruct((wide, cols), F32),
            jax.ShapeDtypeStruct((rank, cols), F32),
        ],
        scratch_shapes=[pltpu.VMEM((cols, tokens), BF16)],
        compiler_params=pltpu.CompilerParams(vmem_limit_bytes=52 * 2**20),
        cost_estimate=pl.CostEstimate(
            flops=2 * tokens * wide * cols, bytes_accessed=2 * tokens * wide, transcendentals=0
        ),
        name="merge",
    )(inputs, grads, errors, basis)


def finish_body(scale, merged, basis, terms, error_next, q_mean, factors):
    @pl.when(pl.program_id(0) == 0)
    def _():
        mean = jnp.sum(terms[...], axis=0) * scale
        q_mean[...] = mean
        high, low = split(mean)
        factors[...] = jnp.concatenate([high, low, high], axis=0)

    high, low = split(basis[...])
    approx = dot(jnp.concatenate([high, high, low], axis=0), factors[...], COLUMNS)
    error_next[...] = (merged[...] - approx).astype(BF16)


def finish(merged, basis, terms, scale, block):
    wide, cols = merged.shape
    rank = basis.shape[0]
    return pl.pallas_call(
        functools.partial(finish_body, scale),
        grid=(wide // block,),
        in_specs=[
            pl.BlockSpec((block, cols), lambda i: (i, 0)),
            pl.BlockSpec((rank, block), lambda i: (0, i)),
            pl.BlockSpec(terms.shape, lambda i: (0, 0, 0)),
        ],
        out_specs=[
            pl.BlockSpec((block, cols), lambda i: (i, 0)),
            pl.BlockSpec((rank, cols), lambda i: (0, 0)),
        ],
        out_shape=[
            jax.ShapeDtypeStruct((wide, cols), BF16),
            jax.ShapeDtypeStruct((rank, cols), F32),
        ],
        scratch_shapes=[pltpu.VMEM((3 * rank, cols), BF16)],
        compiler_params=pltpu.CompilerParams(vmem_limit_bytes=52 * 2**20),
        cost_estimate=pl.CostEstimate(
            flops=6 * rank * wide * cols, bytes_accessed=6 * wide * cols, transcendentals=0
        ),
        name="finish",
    )(merged, basis, terms)


def on_device(normed, key_grad, error_in, q_init):
    inputs, grads, errors = normed[0], key_grad[0], error_in[0]
    tp = lax.axis_size("z")
    plane = lax.axis_size(PLANE)
    replicas = plane * lax.axis_size("c")
    tokens, wide = inputs.shape
    rank = q_init.shape[1]
    gathered = lax.all_gather(inputs, "z", axis=0, tiled=True)

    q_terms = two_terms(q_init.T)
    by_head = fold(lax.dot_general(q_terms, grads, (((1,), (1,)), ((), ())), preferred_element_type=F32))
    by_token = jnp.transpose(by_head.reshape(rank, tp, tokens), (1, 0, 2))
    mine = jnp.sum(swap(by_token, "z"), axis=0)

    p_local = jnp.dot(two_terms(mine), inputs, preferred_element_type=F32)
    p_local += lax.dot_general(q_terms, errors, (((1,), (1,)), ((), ())), preferred_element_type=F32)
    p_local = fold(p_local)
    lanes = 128
    columns = wide // lanes
    halves = plane // columns
    depth = rank // halves
    pieces = jnp.transpose(p_local.reshape(halves, depth, columns, lanes), (0, 2, 1, 3))
    pieces = pieces.reshape(plane, depth, lanes)
    piece = jnp.sum(swap(pieces, PLANE), axis=0)
    piece = jnp.sum(spread(piece, ("c", "z")), axis=0)
    p_sum = spread(piece, PLANE).reshape(halves, columns, depth, lanes)
    p_sum = jnp.transpose(p_sum, (0, 2, 1, 3)).reshape(rank, wide)

    p_basis = jnp.dot(factor(p_sum), p_sum, precision=HIGH)

    merged, q_local = merge(gathered, grads, errors, p_basis, 2048)
    q_local = jnp.sum(spread(q_local.astype(BF16), ("y", "c")).astype(F32), axis=0)
    error_next, q_mean = finish(merged, p_basis, spread(q_local, "x"), 1.0 / replicas, 2048)
    return (error_next[None], p_basis.T, q_mean.T)


def solution(mesh):
    side = math.isqrt(mesh.shape["dp"] // 2)
    whole = Mesh(mesh.devices.reshape(side, side, 2, mesh.shape["tp"]), ("x", "y", "c", "z"))
    dp = ("x", "y", "c")
    placed = (P(dp, "z", None), P(dp, None, "z"), P(dp, None, "z"), P("z", None))
    return jax.shard_map(
        on_device,
        mesh=whole,
        in_specs=placed,
        out_specs=(P(dp, None, "z"), P(), P("z", None)),
        check_vma=False,
    )
```

```python
import functools
import math

import jax
import jax.numpy as jnp
from jax import lax
from jax.experimental import pallas as pl
from jax.experimental.pallas import tpu as pltpu
from jax.sharding import Mesh, PartitionSpec as P

F32 = jnp.float32
BF16 = jnp.bfloat16
HIGH = lax.Precision.HIGHEST
PLANE = ("x", "y")
ROWS = ((1,), (1,))
COLUMNS = ((0,), (0,))
PLAIN = ((1,), (0,))


def fold(value):
    half = value.shape[0] // 2
    return value[:half] + value[half:]


def swap(value, axes):
    return lax.all_to_all(value, axes, 0, 0, tiled=True)


def spread(value, axes):
    return swap(jnp.broadcast_to(value[None], (lax.axis_size(axes),) + value.shape), axes)


def dot(a, b, axes=PLAIN):
    return lax.dot_general(a, b, (axes, ((), ())), preferred_element_type=F32)


def split(value):
    head = value.astype(BF16)
    return head, (value - head.astype(F32)).astype(BF16)


def heads_body(q_turned, grads, out):
    high, low = split(q_turned[...])
    both = jnp.concatenate([high, low], axis=0)
    count, _, rows = out.shape
    for t in range(count):
        out[t] = fold(dot(both, grads[t * rows : (t + 1) * rows, :], ROWS))


def heads(q_turned, grads, count):
    rank = q_turned.shape[0]
    return pl.pallas_call(
        heads_body,
        out_shape=jax.ShapeDtypeStruct((count, rank, grads.shape[0] // count), F32),
        compiler_params=pltpu.CompilerParams(vmem_limit_bytes=56 * 2**20),
        name="heads",
    )(q_turned, grads)


def terms_body(received, q_turned, inputs, errors, out):
    high, low = split(jnp.sum(received[...], axis=0))
    met = jnp.concatenate([high, low], axis=0)
    high, low = split(q_turned[...])
    both = jnp.concatenate([high, low], axis=0)
    count, depth, lanes = out.shape
    columns = inputs.shape[1] // lanes
    wide = 8 * lanes
    for start in range(0, inputs.shape[1], wide):
        part = dot(met, inputs[:, start : start + wide]) + dot(both, errors[start : start + wide, :], ROWS)
        part = fold(part)
        for h in range(count // columns):
            for j in range(wide // lanes):
                piece = part[h * depth : (h + 1) * depth, j * lanes : (j + 1) * lanes]
                out[h * columns + start // lanes + j] = piece


def make_terms(received, q_turned, inputs, errors, count):
    rank, lanes = q_turned.shape
    depth = rank * inputs.shape[1] // (count * lanes)
    return pl.pallas_call(
        terms_body,
        out_shape=jax.ShapeDtypeStruct((count, depth, lanes), F32),
        compiler_params=pltpu.CompilerParams(vmem_limit_bytes=56 * 2**20),
        name="terms",
    )(received, q_turned, inputs, errors)


def basis_body(pieces, basis, again):
    count, depth, lanes = pieces.shape
    rank, wide = basis.shape
    columns = wide // lanes
    value = jnp.concatenate(
        [
            jnp.concatenate([pieces[h * columns + j] for j in range(columns)], axis=1)
            for h in range(count // columns)
        ],
        axis=0,
    )
    left = lax.dot_general(value, value, (ROWS, ((), ())), precision=HIGH, preferred_element_type=F32)
    row = lax.broadcasted_iota(jnp.int32, (rank, rank), 0)
    column = lax.broadcasted_iota(jnp.int32, (rank, rank), 1)
    right = jnp.where(row == column, 1.0, 0.0).astype(F32)
    for k in range(rank):
        scale = lax.rsqrt(left[k : k + 1, k : k + 1])
        upper = left[k : k + 1] * scale
        solved = right[k : k + 1] * scale
        if k + 1 < rank:
            below = jnp.where(row[:, :1] > k, left[:, k : k + 1] * scale, 0.0)
            left = left - below * upper
            right = right - below * solved
        right = jnp.where(row == k, solved, right)
    result = lax.dot_general(right, value, (PLAIN, ((), ())), precision=HIGH, preferred_element_type=F32)
    basis[...] = result
    again[...] = result


def make_basis(pieces, rank):
    count, depth, lanes = pieces.shape
    return pl.pallas_call(
        basis_body,
        out_shape=[jax.ShapeDtypeStruct((rank, count * depth * lanes // rank), F32)] * 2,
        compiler_params=pltpu.CompilerParams(vmem_limit_bytes=12 * 2**20),
        name="basis",
    )(pieces)


def merge_body(inputs, grads, errors, basis, merged, q_out, held, sems):
    count, _, block = held.shape

    def fetch(i):
        return pltpu.make_async_copy(inputs.at[:, pl.ds(i * block, block)], held.at[i], sems.at[i])

    for i in range(count):
        fetch(i).start()
    turned = grads[...].T
    b_high, b_low = split(basis[...])
    rank = b_high.shape[0]
    both = jnp.concatenate([b_high, b_low], axis=0)
    total = jnp.zeros(q_out.shape, F32)
    for i in range(count):
        here = slice(i * block, (i + 1) * block)
        fetch(i).wait()
        part = dot(turned, held[i]).T + errors[here, :].astype(F32)
        merged[here, :] = part
        high, low = split(part)
        total += fold(dot(both[:, here], high)) + dot(b_high[:, here], low)
    q_out[...] = total


def merge(inputs, grads, errors, basis, block):
    tokens, wide = inputs.shape
    cols, rank = grads.shape[1], basis.shape[0]
    count = wide // block
    vmem = pl.BlockSpec(memory_space=pltpu.VMEM)
    return pl.pallas_call(
        merge_body,
        in_specs=[pl.BlockSpec(memory_space=pltpu.HBM), vmem, vmem, vmem],
        out_specs=[vmem, vmem],
        out_shape=[
            jax.ShapeDtypeStruct((wide, cols), F32),
            jax.ShapeDtypeStruct((rank, cols), F32),
        ],
        scratch_shapes=[pltpu.VMEM((count, tokens, block), BF16), pltpu.SemaphoreType.DMA((count,))],
        compiler_params=pltpu.CompilerParams(vmem_limit_bytes=46 * 2**20),
        cost_estimate=pl.CostEstimate(
            flops=2 * tokens * wide * cols, bytes_accessed=2 * tokens * wide, transcendentals=0
        ),
        name="merge",
    )(inputs, grads, errors, basis)


def finish_body(scale, merged, basis, terms, error_next, q_mean, factors):
    @pl.when(pl.program_id(0) == 0)
    def _():
        mean = jnp.sum(terms[...].astype(F32), axis=0) * scale
        q_mean[...] = mean
        high, low = split(mean)
        factors[...] = jnp.concatenate([high, low, high], axis=0)

    high, low = split(basis[...])
    approx = dot(jnp.concatenate([high, high, low], axis=0), factors[...], COLUMNS)
    error_next[...] = (merged[...] - approx).astype(BF16)


def finish(merged, basis, terms, scale, block):
    wide, cols = merged.shape
    rank = basis.shape[0]
    return pl.pallas_call(
        functools.partial(finish_body, scale),
        grid=(wide // block,),
        in_specs=[
            pl.BlockSpec((block, cols), lambda i: (i, 0)),
            pl.BlockSpec((rank, block), lambda i: (0, i)),
            pl.BlockSpec(terms.shape, lambda i: (0, 0, 0)),
        ],
        out_specs=[
            pl.BlockSpec((block, cols), lambda i: (i, 0)),
            pl.BlockSpec((rank, cols), lambda i: (0, 0)),
        ],
        out_shape=[
            jax.ShapeDtypeStruct((wide, cols), BF16),
            jax.ShapeDtypeStruct((rank, cols), F32),
        ],
        scratch_shapes=[pltpu.VMEM((3 * rank, cols), BF16)],
        compiler_params=pltpu.CompilerParams(vmem_limit_bytes=24 * 2**20),
        cost_estimate=pl.CostEstimate(
            flops=6 * rank * wide * cols, bytes_accessed=6 * wide * cols, transcendentals=0
        ),
        name="finish",
    )(merged, basis, terms)


def on_device(normed, key_grad, error_in, q_init):
    inputs, grads, errors = normed[0], key_grad[0], error_in[0]
    tp = lax.axis_size("z")
    plane = lax.axis_size(PLANE)
    replicas = plane * lax.axis_size("c")
    rank = q_init.shape[1]
    gathered = lax.all_gather(inputs, "z", axis=0, tiled=True)

    q_turned = q_init.T
    pieces = make_terms(swap(heads(q_turned, grads, tp), "z"), q_turned, inputs, errors, plane)
    piece = jnp.sum(swap(pieces, PLANE), axis=0)
    piece = jnp.sum(spread(piece, ("c", "z")), axis=0)
    p_basis, basis = make_basis(spread(piece, PLANE), rank)

    merged, q_local = merge(gathered, grads, errors, basis, 2048)
    q_local = jnp.sum(spread(q_local.astype(BF16), ("y", "c")).astype(F32), axis=0)
    q_local = lax.optimization_barrier(q_local).astype(BF16)
    error_next, q_mean = finish(merged, basis, spread(q_local, "x"), 1.0 / replicas, 2048)
    return (error_next[None], p_basis.T, q_mean.T)


def solution(mesh):
    side = math.isqrt(mesh.shape["dp"] // 2)
    whole = Mesh(mesh.devices.reshape(side, side, 2, mesh.shape["tp"]), ("x", "y", "c", "z"))
    dp = ("x", "y", "c")
    placed = (P(dp, "z", None), P(dp, None, "z"), P(dp, None, "z"), P("z", None))
    return jax.shard_map(
        on_device,
        mesh=whole,
        in_specs=placed,
        out_specs=(P(dp, None, "z"), P(), P("z", None)),
        check_vma=False,
    )
```

```python
import functools
import math

import jax
import jax.numpy as jnp
from jax import lax
from jax.experimental import pallas as pl
from jax.experimental.pallas import tpu as pltpu
from jax.sharding import Mesh, PartitionSpec as P

F32 = jnp.float32
BF16 = jnp.bfloat16
HIGH = lax.Precision.HIGHEST
PLANE = ("x", "y")
ROWS = ((1,), (1,))
COLUMNS = ((0,), (0,))
PLAIN = ((1,), (0,))


def fold(value):
    half = value.shape[0] // 2
    return value[:half] + value[half:]


def swap(value, axes):
    return lax.all_to_all(value, axes, 0, 0, tiled=True)


def spread(value, axes):
    return swap(jnp.broadcast_to(value[None], (lax.axis_size(axes),) + value.shape), axes)


def dot(a, b, axes=PLAIN):
    return lax.dot_general(a, b, (axes, ((), ())), preferred_element_type=F32)


def split(value):
    head = value.astype(BF16)
    return head, (value - head.astype(F32)).astype(BF16)


def heads_body(q_turned, grads, side, out, passed):
    passed[...] = side[...]
    high, low = split(q_turned[...])
    both = jnp.concatenate([high, low], axis=0)
    count, _, rows = out.shape
    for t in range(count):
        out[t] = fold(dot(both, grads[t * rows : (t + 1) * rows, :], ROWS))


def heads(q_turned, grads, side, count):
    rank = q_turned.shape[0]
    return pl.pallas_call(
        heads_body,
        out_shape=[
            jax.ShapeDtypeStruct((count, rank, grads.shape[0] // count), F32),
            jax.ShapeDtypeStruct(side.shape, F32),
        ],
        compiler_params=pltpu.CompilerParams(vmem_limit_bytes=56 * 2**20),
        name="heads",
    )(q_turned, grads, side)


def terms_body(received, q_turned, inputs, errors, side, kept, given):
    high, low = split(jnp.sum(received[...], axis=0))
    met = jnp.concatenate([high, low], axis=0)
    high, low = split(q_turned[...])
    both = jnp.concatenate([high, low], axis=0)
    count, depth, lanes = kept.shape
    first = side[...] == 0.0
    columns = inputs.shape[1] // lanes
    wide = 8 * lanes
    for start in range(0, inputs.shape[1], wide):
        part = dot(met, inputs[:, start : start + wide]) + dot(both, errors[start : start + wide, :], ROWS)
        part = fold(part)
        for h in range(count // columns):
            for j in range(wide // lanes):
                piece = part[2 * h * depth : 2 * (h + 1) * depth, j * lanes : (j + 1) * lanes]
                place = h * columns + start // lanes + j
                kept[place] = jnp.where(first, piece[:depth], piece[depth:])
                given[place] = jnp.where(first, piece[depth:], piece[:depth])


def make_terms(received, q_turned, inputs, errors, side, count):
    rank, lanes = q_turned.shape
    depth = rank * inputs.shape[1] // (2 * count * lanes)
    return pl.pallas_call(
        terms_body,
        out_shape=[jax.ShapeDtypeStruct((count, depth, lanes), F32)] * 2,
        compiler_params=pltpu.CompilerParams(vmem_limit_bytes=56 * 2**20),
        name="terms",
    )(received, q_turned, inputs, errors, side)


def basis_body(own, other, side, basis, again):
    count, _, lanes = own.shape
    rank, wide = basis.shape
    first = side[...] == 0.0
    upper = [jnp.where(first, own[i], other[i]) for i in range(count)]
    lower = [jnp.where(first, other[i], own[i]) for i in range(count)]
    columns = wide // lanes
    value = jnp.concatenate(
        [
            jnp.concatenate([half[h * columns + j] for j in range(columns)], axis=1)
            for h in range(count // columns)
            for half in (upper, lower)
        ],
        axis=0,
    )
    left = lax.dot_general(value, value, (ROWS, ((), ())), precision=HIGH, preferred_element_type=F32)
    row = lax.broadcasted_iota(jnp.int32, (rank, rank), 0)
    column = lax.broadcasted_iota(jnp.int32, (rank, rank), 1)
    right = jnp.where(row == column, 1.0, 0.0).astype(F32)
    for k in range(rank):
        scale = lax.rsqrt(left[k : k + 1, k : k + 1])
        upper = left[k : k + 1] * scale
        solved = right[k : k + 1] * scale
        if k + 1 < rank:
            below = jnp.where(row[:, :1] > k, left[:, k : k + 1] * scale, 0.0)
            left = left - below * upper
            right = right - below * solved
        right = jnp.where(row == k, solved, right)
    result = lax.dot_general(right, value, (PLAIN, ((), ())), precision=HIGH, preferred_element_type=F32)
    basis[...] = result
    again[...] = result


def make_basis(own, other, side, rank):
    wide = 2 * own.size // rank
    return pl.pallas_call(
        basis_body,
        out_shape=[jax.ShapeDtypeStruct((rank, wide), F32)] * 2,
        compiler_params=pltpu.CompilerParams(vmem_limit_bytes=12 * 2**20),
        name="basis",
    )(own, other, side)


def merge_body(inputs, grads, errors, basis, merged, q_out, held, sems):
    count, _, block = held.shape

    def fetch(i):
        return pltpu.make_async_copy(inputs.at[:, pl.ds(i * block, block)], held.at[i], sems.at[i])

    for i in range(count):
        fetch(i).start()
    turned = grads[...].T
    b_high, b_low = split(basis[...])
    rank = b_high.shape[0]
    both = jnp.concatenate([b_high, b_low], axis=0)
    total = jnp.zeros(q_out.shape, F32)
    for i in range(count):
        here = slice(i * block, (i + 1) * block)
        fetch(i).wait()
        part = dot(turned, held[i]).T + errors[here, :].astype(F32)
        merged[here, :] = part
        high, low = split(part)
        total += fold(dot(both[:, here], high)) + dot(b_high[:, here], low)
    q_out[...] = total


def merge(inputs, grads, errors, basis, block):
    tokens, wide = inputs.shape
    cols, rank = grads.shape[1], basis.shape[0]
    count = wide // block
    vmem = pl.BlockSpec(memory_space=pltpu.VMEM)
    return pl.pallas_call(
        merge_body,
        in_specs=[pl.BlockSpec(memory_space=pltpu.HBM), vmem, vmem, vmem],
        out_specs=[vmem, vmem],
        out_shape=[
            jax.ShapeDtypeStruct((wide, cols), F32),
            jax.ShapeDtypeStruct((rank, cols), F32),
        ],
        scratch_shapes=[pltpu.VMEM((count, tokens, block), BF16), pltpu.SemaphoreType.DMA((count,))],
        compiler_params=pltpu.CompilerParams(vmem_limit_bytes=46 * 2**20),
        cost_estimate=pl.CostEstimate(
            flops=2 * tokens * wide * cols, bytes_accessed=2 * tokens * wide, transcendentals=0
        ),
        name="merge",
    )(inputs, grads, errors, basis)


def finish_body(scale, merged, basis, terms, error_next, q_mean, factors):
    @pl.when(pl.program_id(0) == 0)
    def _():
        mean = jnp.sum(terms[...].astype(F32), axis=0) * scale
        q_mean[...] = mean
        high, low = split(mean)
        factors[...] = jnp.concatenate([high, low, high], axis=0)

    high, low = split(basis[...])
    approx = dot(jnp.concatenate([high, high, low], axis=0), factors[...], COLUMNS)
    error_next[...] = (merged[...] - approx).astype(BF16)


def finish(merged, basis, terms, scale, block):
    wide, cols = merged.shape
    rank = basis.shape[0]
    return pl.pallas_call(
        functools.partial(finish_body, scale),
        grid=(wide // block,),
        in_specs=[
            pl.BlockSpec((block, cols), lambda i: (i, 0)),
            pl.BlockSpec((rank, block), lambda i: (0, i)),
            pl.BlockSpec(terms.shape, lambda i: (0, 0, 0)),
        ],
        out_specs=[
            pl.BlockSpec((block, cols), lambda i: (i, 0)),
            pl.BlockSpec((rank, cols), lambda i: (0, 0)),
        ],
        out_shape=[
            jax.ShapeDtypeStruct((wide, cols), BF16),
            jax.ShapeDtypeStruct((rank, cols), F32),
        ],
        scratch_shapes=[pltpu.VMEM((3 * rank, cols), BF16)],
        compiler_params=pltpu.CompilerParams(vmem_limit_bytes=24 * 2**20),
        cost_estimate=pl.CostEstimate(
            flops=6 * rank * wide * cols, bytes_accessed=6 * wide * cols, transcendentals=0
        ),
        name="finish",
    )(merged, basis, terms)


def on_device(normed, key_grad, error_in, q_init):
    inputs, grads, errors = normed[0], key_grad[0], error_in[0]
    tp = lax.axis_size("z")
    plane = lax.axis_size(PLANE)
    replicas = plane * lax.axis_size("c")
    rank = q_init.shape[1]
    gathered = lax.all_gather(inputs, "z", axis=0, tiled=True)

    q_turned = q_init.T
    side = jnp.full((8, 128), lax.axis_index("c").astype(F32))
    by_token, side = heads(q_turned, grads, side, tp)
    kept, given = make_terms(swap(by_token, "z"), q_turned, inputs, errors, side, plane)
    cross = [(0, 1), (1, 0)]
    piece = jnp.sum(swap(kept + lax.ppermute(given, "c", cross), PLANE), axis=0)
    piece = jnp.sum(spread(piece, "z"), axis=0)
    half = spread(piece, PLANE)
    p_basis, basis = make_basis(half, lax.ppermute(half, "c", cross), side, rank)

    merged, q_local = merge(gathered, grads, errors, basis, 2048)
    q_local = jnp.sum(spread(q_local.astype(BF16), ("y", "c")).astype(F32), axis=0)
    q_local = lax.optimization_barrier(q_local).astype(BF16)
    error_next, q_mean = finish(merged, basis, spread(q_local, "x"), 1.0 / replicas, 2048)
    return (error_next[None], p_basis.T, q_mean.T)


def solution(mesh):
    side = math.isqrt(mesh.shape["dp"] // 2)
    whole = Mesh(mesh.devices.reshape(side, side, 2, mesh.shape["tp"]), ("x", "y", "c", "z"))
    dp = ("x", "y", "c")
    placed = (P(dp, "z", None), P(dp, None, "z"), P(dp, None, "z"), P("z", None))
    return jax.shard_map(
        on_device,
        mesh=whole,
        in_specs=placed,
        out_specs=(P(dp, None, "z"), P(), P("z", None)),
        check_vma=False,
    )
```
